32 devices in a mesh: chan: 16 (over z, y, core), seg: 2 (over x).
Axes of the slice: x: 2, y: 2, z: 4, core: 2. Of those that a mesh axis runs over, the one named last changes fastest.
Arguments:
- signal: bfloat16 [16, 1024, 4096], P('seg', None, 'chan'), may hold values from -150 to 150
- band: int32 [16, 4], replicated, may hold values from 0 to 192
- sched: int32 [16, 4], P('chan'), may hold values 0 or 1
Outputs:
- cross: bfloat16 [16, 4, 2, 64, 256, 256], P('chan', None, None, 'seg')
The draws below stay inside these ranges and needn't reach their ends.
All inputs are finite; a program needn't handle non-finite values. No bound on the sum of `sched` on one device may be relied on, other than what follows from the above.
Results may differ from the reference program's by a relative error of at most 0.0067.
Values may be sent and summed in bfloat16 or wider, within the bound.
No kernel may reach another device: no remote copies, remote signals or barrier semaphores. Data moves between devices by JAX's collectives and lax.ppermute only.
A program may use at most 192 MiB of HBM per device.

```python
import math
import jax
import jax.numpy as jnp
from jax import lax

CB = 256
L = 1024
NB = 256
BW = 64
PAIRS = 4
BLOCKS = 16
CH = 4096
SEGS = 16


def draw_signal(key, part):
    key = jax.random.fold_in(key, 11)
    key_base, key_scale = jax.random.split(key, 2)
    segment = jnp.arange(SEGS, dtype=jnp.float32)[:, None, None]
    span = max(SEGS - 1, 1)
    base = jax.random.truncated_normal(key_base, -4.0, 4.0, (SEGS, L, CH), jnp.float32)
    envelope = 1.0 + 2.0 * segment / span
    scales = jnp.exp(jax.random.uniform(key_scale, (1, 1, CH), jnp.float32) * math.log(10.0))
    return (base * envelope * scales).astype(jnp.bfloat16)


def with_ends(drawn, stream_key, least, high):
    shape = drawn.shape
    index_at = [jax.random.randint(jax.random.fold_in(stream_key, axis), (), 0, shape[axis]) for axis in range(len(shape))]
    drawn = drawn.at[tuple(index_at)].set(least)
    longest = shape.index(max(shape))
    index_at[longest] = (index_at[longest] + 1) % shape[longest]
    return drawn.at[tuple(index_at)].set(high)


def setup_inputs(seed: int = 0) -> dict:
    key_list = jax.random.split(jax.random.key(seed), 4)
    signal = draw_signal(jax.random.fold_in(key_list[3], 71), 0)
    band = with_ends(jax.random.randint(key_list[1], (BLOCKS, PAIRS), 0, NB - BW + 1), jax.random.fold_in(key_list[1], 1), 0, NB - BW).astype(jnp.int32)
    sched = with_ends((jax.random.randint(key_list[2], (BLOCKS, PAIRS), 0, 2) < 1).astype(jnp.int32), jax.random.fold_in(key_list[2], 1), 0, 1)
    return dict(signal=signal, band=band, sched=sched)


def dft_table(nbins, length):
    freq = jnp.arange(nbins, dtype=jnp.int32)[:, None]
    sample = jnp.arange(length, dtype=jnp.int32)[None, :]
    phase = (freq * sample % length).astype(jnp.float32) * (2.0 * math.pi / length)
    window = 0.5 - 0.5 * jnp.cos(sample.astype(jnp.float32) * (2.0 * math.pi / length))
    return jnp.stack([window * jnp.cos(phase), -window * jnp.sin(phase)]).astype(jnp.bfloat16)

def pair_cross(first, second):
    first = first.astype(jnp.float32)
    second = second.astype(jnp.float32)
    real_part = jnp.einsum('sfi,sfj->fij', first[:, 0], second[:, 0]) + jnp.einsum('sfi,sfj->fij', first[:, 1], second[:, 1])
    imag_part = jnp.einsum('sfi,sfj->fij', first[:, 1], second[:, 0]) - jnp.einsum('sfi,sfj->fij', first[:, 0], second[:, 1])
    return jnp.stack([real_part, imag_part])

def reference(signal, band, sched):
    power = lax.optimization_barrier(jnp.sum(jnp.square(signal.astype(jnp.float32)), axis=(0, 1)))
    inv_rms = lax.rsqrt(power / (SEGS * L) + 1e-06)
    table = dft_table(NB, L)
    raw = jnp.einsum('rfl,slc->srfc', table.astype(jnp.float32), signal.astype(jnp.float32))
    spectra = (raw * inv_rms).astype(jnp.bfloat16)
    blocked = spectra.reshape(SEGS, 2, NB, BLOCKS, CB)
    scale = 1.0 / (SEGS * 0.375 * L)

    def one_block(block):
        own_all = lax.dynamic_index_in_dim(blocked, block, 3, keepdims=False)
        results = []
        for pair in range(PAIRS):
            offset = band[block, pair]
            neighbour = ((block + pair) % BLOCKS).astype(jnp.int32)
            other_all = lax.dynamic_index_in_dim(blocked, neighbour, 3, keepdims=False)
            own = lax.dynamic_slice_in_dim(own_all, offset, BW, 2)
            other = lax.dynamic_slice_in_dim(other_all, offset, BW, 2)
            live = sched[block, pair].astype(jnp.float32)
            results.append((pair_cross(own, other) * scale * live).astype(jnp.bfloat16))
        return jnp.stack(results)
    return lax.map(one_block, jnp.arange(BLOCKS, dtype=jnp.int32))
```

```python
import functools

import jax
import jax.numpy as jnp
import ml_dtypes
import numpy as np
from jax import lax
from jax.experimental import pallas as pl
from jax.experimental.pallas import tpu as pltpu
from jax.sharding import PartitionSpec as P

NB = 256
BW = 64
PAIRS = 4
LANES = 128
LIFT = 1024.0


def dft_table(nbins, length):
    freq = np.arange(nbins)[:, None]
    sample = np.arange(length)[None, :]
    phase = (freq * sample % length) * (2.0 * np.pi / length)
    window = 0.5 - 0.5 * np.cos(sample * (2.0 * np.pi / length))
    table = np.concatenate([window * np.cos(phase), -window * np.sin(phase)])
    return (table.astype(np.float32).astype(ml_dtypes.bfloat16).astype(np.float32) * LIFT).astype(ml_dtypes.bfloat16)


def window_plan(seg):
    own = [(pair, False, shift) for pair in range(PAIRS) for shift in range(seg)]
    lent = [(pair, True, shift) for pair in range(1, PAIRS) for shift in range(seg)]
    return sorted(own + lent, key=lambda w: (w[0], -w[2], w[1]))


def carries_power(window):
    pair, lent, _ = window
    return lent or pair == 0


def split3(x):
    high = x.astype(jnp.bfloat16)
    rest = x - high.astype(jnp.float32)
    mid = rest.astype(jnp.bfloat16)
    low = (rest - mid.astype(jnp.float32)).astype(jnp.bfloat16)
    return high, mid, low


def spectra_kernel(plan, chan, seg, band_ref, table_hbm, signal_hbm, *refs):
    n = len(plan)
    outs, (table, signal, raw, cut, table_sem, signal_sem, out_sem) = refs[:n], refs[n:]
    segs, _, width = signal.shape
    nbins = table.shape[0] // 2
    rows = 2 * segs
    bins = BW // seg
    table_copy = pltpu.make_async_copy(table_hbm, table, table_sem)
    signal_copy = pltpu.make_async_copy(signal_hbm, signal, signal_sem)
    table_copy.start()
    signal_copy.start()
    block, seat = lax.axis_index("chan"), lax.axis_index("seg")
    table_copy.wait()
    signal_copy.wait()
    power = jnp.zeros((8, width), jnp.float32)
    for s in range(segs):
        spectrum = jnp.dot(table[...], signal[s], preferred_element_type=jnp.float32)
        for r in range(2):
            for h in range(width // LANES):
                raw[h, pl.ds(r * segs + s, nbins, stride=rows), :] = spectrum[r * nbins : (r + 1) * nbins, h * LANES : (h + 1) * LANES]
        x = signal[s].astype(jnp.float32)
        power = power + jnp.sum((x * x).reshape(-1, 8, width), axis=0)
    parts = split3(jnp.sum(power, axis=0, keepdims=True))
    row = lax.broadcasted_iota(jnp.int32, (rows, width), 0)
    packed = jnp.zeros((rows, width), jnp.float32)
    for i, part in enumerate(parts):
        packed = jnp.where(row == i, part.astype(jnp.float32), packed)
    packed = packed.astype(jnp.bfloat16)
    copies = []
    for k, (pair, lent, shift) in enumerate(plan):
        user = lax.rem(block + (chan - pair), chan) if lent else block
        first = band_ref[user, pair] + lax.rem(seat + shift, seg) * bins
        start = pl.multiple_of(first * rows, rows)
        for h in range(width // LANES):
            piece = raw[h, pl.ds(start, bins * rows), :].reshape(bins, rows, LANES)
            cut[k, :bins, :, h * LANES : (h + 1) * LANES] = piece.astype(jnp.bfloat16)
        size = bins
        if carries_power(plan[k]):
            cut[k, bins] = packed
            size = bins + 1
        copy = pltpu.make_async_copy(cut.at[k, pl.ds(0, size)], outs[k], out_sem.at[k])
        copy.start()
        copies.append(copy)
    for copy in copies:
        copy.wait()


def cut_spectra(plan, chan, seg, band, table, signal):
    segs, length, width = signal.shape
    rows, bins, n = 2 * segs, BW // seg, len(plan)
    anywhere = pl.BlockSpec(memory_space=pl.ANY)
    return pl.pallas_call(
        functools.partial(spectra_kernel, plan, chan, seg),
        in_specs=[pl.BlockSpec(memory_space=pltpu.SMEM), anywhere, anywhere],
        out_specs=[anywhere] * n,
        out_shape=[jax.ShapeDtypeStruct((bins + carries_power(w), rows, width), jnp.bfloat16) for w in plan],
        scratch_shapes=[
            pltpu.VMEM(table.shape, jnp.bfloat16),
            pltpu.VMEM(signal.shape, jnp.bfloat16),
            pltpu.VMEM((width // LANES, table.shape[0] * segs, LANES), jnp.float32),
            pltpu.VMEM((n, bins + 1, rows, width), jnp.bfloat16),
            pltpu.SemaphoreType.DMA,
            pltpu.SemaphoreType.DMA,
            pltpu.SemaphoreType.DMA((n,)),
        ],
        compiler_params=pltpu.CompilerParams(vmem_limit_bytes=56 << 20),
    )(band, table, signal)


def turned(x):
    half = x.shape[1] // 2
    return jnp.concatenate([x[:, half:], -x[:, :half]], axis=1)


def inv_rms_of(tiles, samples):
    power = 0.0
    for tile in tiles:
        t = tile[0].astype(jnp.float32)
        power = power + (t[0:1] + t[1:2] + t[2:3])
    return lax.rsqrt(power / samples + 1e-06)


def cross_kernel(pair, seg, samples, scale, sched_ref, *refs):
    mine, theirs = refs[:seg], refs[seg : 2 * seg]
    my_power, their_power = refs[2 * seg : 3 * seg], refs[3 * seg : 4 * seg]
    out, by_row, by_column = refs[-3:]
    bins, _, width = mine[0].shape
    live = sched_ref[0, pair]

    @pl.when(live == 0)
    def _():
        out[...] = jnp.zeros(out.shape, out.dtype)

    @pl.when((live != 0) & (pl.program_id(0) == 0))
    def _():
        by_row[...] = jnp.broadcast_to(inv_rms_of(my_power, samples) * scale, (width, width)).T
        by_column[...] = inv_rms_of(their_power, samples)

    @pl.when(live != 0)
    def _():
        for f in range(bins):
            x = jnp.concatenate([m[f] for m in mine], axis=0)
            xt = jnp.concatenate([turned(m[f : f + 1])[0] for m in mine], axis=0)
            y = jnp.concatenate([t[f] for t in theirs], axis=0)
            for r, first in enumerate((x, xt)):
                product = lax.dot_general(first, y, (((0,), (0,)), ((), ())), preferred_element_type=jnp.float32)
                out[0, 0, r, f] = (product * by_row[...] * by_column[...]).astype(out.dtype)


def cross(pair, seg, samples, scale, sched, mine, theirs, my_power, their_power, shape, out):
    rows, width = mine[0].shape[1:]
    total = shape[3]
    bins = min(16, total)
    block = pl.BlockSpec((bins, rows, width), lambda i, sched: (i, 0, 0))
    tile = pl.BlockSpec((1, rows, width), lambda i, sched: (total, 0, 0))
    operands = [sched, *mine, *theirs, *my_power, *their_power]
    in_specs = [block] * (2 * seg) + [tile] * (2 * seg)
    aliases = {}
    if out is not None:
        aliases = {len(operands): 0}
        operands.append(out)
        in_specs.append(pl.BlockSpec(memory_space=pl.ANY))
    return pl.pallas_call(
        functools.partial(cross_kernel, pair, seg, samples, scale),
        grid_spec=pltpu.PrefetchScalarGridSpec(
            num_scalar_prefetch=1,
            grid=(total // bins,),
            in_specs=in_specs,
            out_specs=pl.BlockSpec((1, 1, 2, bins, width, width), lambda i, sched: (0, pair, 0, i, 0, 0)),
            scratch_shapes=[pltpu.VMEM((width, width), jnp.float32), pltpu.VMEM((1, width), jnp.float32)],
        ),
        out_shape=jax.ShapeDtypeStruct(shape, jnp.bfloat16),
        input_output_aliases=aliases,
        compiler_params=pltpu.CompilerParams(vmem_limit_bytes=56 << 20),
        cost_estimate=pl.CostEstimate(
            flops=4 * total * seg * rows * width * width, bytes_accessed=4 * total * width * width, transcendentals=0
        ),
    )(*operands)


def body(signal, band, sched):
    seg_dev, length, width = signal.shape
    seg, chan = lax.axis_size("seg"), lax.axis_size("chan")
    segs = seg_dev * seg
    plan = window_plan(seg)
    table = jnp.asarray(dft_table(NB, length))
    cuts = dict(zip(plan, cut_spectra(plan, chan, seg, band, table, signal)))

    def delivered(window):
        pair, lent, shift = window
        away = pair if lent else 0
        if not away and not shift:
            return cuts[window]
        route = [(c * seg + s, (c - away) % chan * seg + (s + shift) % seg) for c in range(chan) for s in range(seg)]
        return lax.ppermute(cuts[window], ("chan", "seg"), route)

    arrived = {window: delivered(window) for window in plan}
    scale = 1.0 / (segs * 0.375 * length) / LIFT**2
    shape = (1, PAIRS, 2, BW // seg, width, width)
    my_power = [arrived[0, False, k] for k in range(seg)]
    out = None
    for pair in range(PAIRS):
        mine = [arrived[pair, False, k] for k in range(seg)]
        theirs = [arrived[pair, True, k] for k in range(seg)] if pair else mine
        their_power = theirs if pair else my_power
        out = cross(pair, seg, segs * length, scale, sched, mine, theirs, my_power, their_power, shape, out)
    return out


def solution(mesh):
    in_specs = (P("seg", None, "chan"), P(), P("chan", None))
    out_specs = P("chan", None, None, "seg", None, None)
    return jax.shard_map(body, mesh=mesh, in_specs=in_specs, out_specs=out_specs, check_vma=False)
```

```python
import functools

import jax
import jax.numpy as jnp
import ml_dtypes
import numpy as np
from jax import lax
from jax.experimental import pallas as pl
from jax.experimental.pallas import tpu as pltpu
from jax.sharding import PartitionSpec as P

NB = 256
BW = 64
PAIRS = 4
LANES = 128
LIFT = 1024.0
CROSS_VMEM = 20 << 20


def dft_table(nbins, length):
    freq = np.arange(nbins)[:, None]
    sample = np.arange(length)[None, :]
    phase = (freq * sample % length) * (2.0 * np.pi / length)
    window = 0.5 - 0.5 * np.cos(sample * (2.0 * np.pi / length))
    table = np.concatenate([window * np.cos(phase), -window * np.sin(phase)])
    return (table.astype(np.float32).astype(ml_dtypes.bfloat16).astype(np.float32) * LIFT).astype(ml_dtypes.bfloat16)


def message_plan(seg):
    away = range(1, seg)
    plan = [((0, 1), False, k, True) for k in away]
    plan += [((1,), True, k, True) for k in away]
    plan += [((pair,), True, 0, True) for pair in range(1, PAIRS)]
    plan += [((2, 3), False, k, False) for k in away]
    plan += [((pair,), True, k, True) for pair in (2, 3) for k in away]
    return plan + [(tuple(range(PAIRS)), False, 0, True)]


def waits_for(message, seg):
    pairs, lent, shift, _ = message
    own = ((0, 1), False, shift, True)
    near = [((pair,), True, 0, True) for pair in range(1, PAIRS)]
    across = ((1,), True, shift, True)
    if pairs == (2, 3):
        return [own, *near[:2]]
    if pairs == (2,) and lent and shift:
        return [across]
    if pairs == (3,) and lent and shift:
        return [across]
    return []


def split3(x):
    high = x.astype(jnp.bfloat16)
    rest = x - high.astype(jnp.float32)
    mid = rest.astype(jnp.bfloat16)
    low = (rest - mid.astype(jnp.float32)).astype(jnp.bfloat16)
    return high, mid, low


def first_bin(band_ref, pair, lent, shift, seg):
    block, seat, chan = lax.axis_index("chan"), lax.axis_index("seg"), band_ref.shape[1]
    user = lax.rem(block + (chan - pair), chan) if lent else block
    return band_ref[pair, user] + lax.rem(seat + shift, seg) * (BW // seg)


def spectra_kernel(plan, seg, band_ref, table_hbm, signal_hbm, *refs):
    n = len(plan)
    outs, (table, signal, raw, spectra, table_sem, signal_sem, out_sem) = refs[:n], refs[n:]
    segs, _, width = signal.shape
    nbins = table.shape[0] // 2
    rows = 2 * segs
    bins = BW // seg
    table_copy = pltpu.make_async_copy(table_hbm, table, table_sem)
    signal_copy = pltpu.make_async_copy(signal_hbm, signal, signal_sem)
    table_copy.start()
    signal_copy.start()
    table_copy.wait()
    signal_copy.wait()
    power = jnp.zeros((8, width), jnp.float32)
    for s in range(segs):
        spectrum = jnp.dot(table[...], signal[s], preferred_element_type=jnp.float32)
        for r in range(2):
            for h in range(width // LANES):
                raw[h, pl.ds(r * segs + s, nbins, stride=rows), :] = spectrum[r * nbins : (r + 1) * nbins, h * LANES : (h + 1) * LANES]
        x = signal[s].astype(jnp.float32)
        power = power + jnp.sum((x * x).reshape(-1, 8, width), axis=0)
    parts = split3(jnp.sum(power, axis=0, keepdims=True))
    row = lax.broadcasted_iota(jnp.int32, (rows, width), 0)
    packed = jnp.zeros((rows, width), jnp.float32)
    for i, part in enumerate(parts):
        packed = jnp.where(row == i, part.astype(jnp.float32), packed)
    spectra[nbins] = packed.astype(jnp.bfloat16)
    for h in range(width // LANES):
        spectra[:nbins, :, h * LANES : (h + 1) * LANES] = raw[h].reshape(nbins, rows, LANES).astype(jnp.bfloat16)
    copies = []
    for (pairs, lent, shift, powered), out in zip(plan, outs):
        pieces = [(first_bin(band_ref, pair, lent, shift, seg), bins) for pair in pairs] + [(nbins, 1)] * powered
        for i, (start, size) in enumerate(pieces):
            copies.append(pltpu.make_async_copy(spectra.at[pl.ds(start, size)], out.at[pl.ds(i * bins, size)], out_sem.at[len(copies)]))
    for copy in copies:
        copy.start()
    for copy in copies:
        copy.wait()


def message_shape(message, bins, rows, width):
    pairs, _, _, powered = message
    return jax.ShapeDtypeStruct((len(pairs) * bins + powered, rows, width), jnp.bfloat16)


def make_spectra(plan, seg, band, table, signal):
    segs, length, width = signal.shape
    rows, bins, n, nbins = 2 * segs, BW // seg, len(plan), table.shape[0] // 2
    anywhere = pl.BlockSpec(memory_space=pl.ANY)
    return pl.pallas_call(
        functools.partial(spectra_kernel, plan, seg),
        in_specs=[pl.BlockSpec(memory_space=pltpu.SMEM), anywhere, anywhere],
        out_specs=[anywhere] * n,
        out_shape=[message_shape(m, bins, rows, width) for m in plan],
        scratch_shapes=[
            pltpu.VMEM(table.shape, jnp.bfloat16),
            pltpu.VMEM(signal.shape, jnp.bfloat16),
            pltpu.VMEM((width // LANES, nbins * rows, LANES), jnp.float32),
            pltpu.VMEM((nbins + 1, rows, width), jnp.bfloat16),
            pltpu.SemaphoreType.DMA,
            pltpu.SemaphoreType.DMA,
            pltpu.SemaphoreType.DMA((sum(len(m[0]) + m[3] for m in plan),)),
        ],
        compiler_params=pltpu.CompilerParams(vmem_limit_bytes=56 << 20),
    )(band, table, signal)


def turned(y):
    half = y.shape[0] // 2
    return jnp.concatenate([-y[half:], y[:half]], axis=0)


def inv_rms_of(tiles, samples):
    power = 0.0
    for tile in tiles:
        t = tile.astype(jnp.float32)
        power = power + (t[0:1] + t[1:2] + t[2:3])
    return lax.rsqrt(power / samples + 1e-06)


def cross_kernel(pair, firsts, samples, scale, sched_ref, *refs):
    n = len(firsts)
    arrays, (out, held, ring, weight, in_sem, out_sem) = refs[:n], refs[-6:]
    _, bins, _, width = held.shape
    depth, _, chunk = ring.shape[:3]
    steps = bins // chunk
    out_copies = [
        pltpu.make_async_copy(ring.at[c % depth], out.at[0, pair, :, pl.ds(c * chunk, chunk)], out_sem.at[c]) for c in range(steps)
    ]
    zero_copies = [pltpu.make_async_copy(ring.at[0], out.at[0, pair, :, pl.ds(c * chunk, chunk)], out_sem.at[c]) for c in range(steps)]
    live = sched_ref[0, pair]

    @pl.when(live == 0)
    def _():
        ring[0] = jnp.zeros(ring.shape[1:], ring.dtype)
        for copy in zero_copies:
            copy.start()
        for copy in zero_copies:
            copy.wait()

    @pl.when(live != 0)
    def _():
        copies = [
            pltpu.make_async_copy(array.at[pl.ds(first, size)], held.at[k, pl.ds(0, size)], in_sem.at[k])
            for k, (array, (first, size)) in enumerate(zip(arrays, firsts))
        ]
        for copy in copies:
            copy.start()
        for copy in copies:
            copy.wait()
        tiles = [k for k in range(n) if firsts[k][1] == 1]
        blocks = [k for k in range(n) if firsts[k][1] != 1]
        halves = 2 if pair else 1
        mine, theirs = blocks[: len(blocks) // halves], blocks[-(len(blocks) // halves) :]
        my_power, their_power = tiles[: len(tiles) // halves], tiles[-(len(tiles) // halves) :]
        by_row = jnp.broadcast_to(inv_rms_of([held[k, 0] for k in my_power], samples) * scale, (width, width)).T
        weight[...] = by_row * inv_rms_of([held[k, 0] for k in their_power], samples)
        for c in range(steps):
            if c >= depth:
                out_copies[c - depth].wait()
            for f in range(c * chunk, (c + 1) * chunk):
                x = jnp.concatenate([held[k, f] for k in mine], axis=0)
                y = jnp.concatenate([held[k, f] for k in theirs], axis=0)
                y_turned = jnp.concatenate([turned(held[k, f]) for k in theirs], axis=0)
                partner = jnp.concatenate([y, y_turned], axis=1)
                product = lax.dot_general(x, partner, (((0,), (0,)), ((), ())), preferred_element_type=jnp.float32)
                for r in range(2):
                    part = product[:, r * width : (r + 1) * width] * weight[...]
                    ring[c % depth, r, f - c * chunk] = part.astype(ring.dtype)
            out_copies[c].start()
        for c in range(max(steps - depth, 0), steps):
            out_copies[c].wait()


def cross(pair, samples, scale, sched, mine, theirs, my_power, their_power, shape, out):
    rows, width = mine[0][0].shape[1:]
    bins = shape[3]
    chunk = min(4, bins)
    blocks = mine + theirs if pair else mine
    tiles = my_power + their_power if pair else my_power
    arrays = [array for array, _ in blocks] + tiles
    firsts = [(first, bins) for _, first in blocks] + [(array.shape[0] - 1, 1) for array in tiles]
    anywhere = pl.BlockSpec(memory_space=pl.ANY)
    operands = [sched, *arrays]
    aliases = {}
    if out is not None:
        aliases = {len(operands): 0}
        operands.append(out)
    return pl.pallas_call(
        functools.partial(cross_kernel, pair, firsts, samples, scale),
        in_specs=[pl.BlockSpec(memory_space=pltpu.SMEM)] + [anywhere] * (len(operands) - 1),
        out_specs=anywhere,
        scratch_shapes=[
            pltpu.VMEM((len(firsts), bins, rows, width), jnp.bfloat16),
            pltpu.VMEM((4, 2, chunk, width, width), jnp.bfloat16),
            pltpu.VMEM((width, width), jnp.float32),
            pltpu.SemaphoreType.DMA((len(firsts),)),
            pltpu.SemaphoreType.DMA((bins // chunk,)),
        ],
        out_shape=jax.ShapeDtypeStruct(shape, jnp.bfloat16),
        input_output_aliases=aliases,
        compiler_params=pltpu.CompilerParams(vmem_limit_bytes=CROSS_VMEM),
        cost_estimate=pl.CostEstimate(
            flops=4 * bins * len(mine) * rows * width * width, bytes_accessed=4 * bins * width * width, transcendentals=0
        ),
    )(*operands)


def body(signal, band, sched):
    seg_dev, length, width = signal.shape
    seg, chan = lax.axis_size("seg"), lax.axis_size("chan")
    segs = seg_dev * seg
    bins = BW // seg
    plan = message_plan(seg)
    table = jnp.asarray(dft_table(NB, length))
    cuts = make_spectra(plan, seg, band.T, table, signal)

    def delivered(message, cut):
        pairs, lent, shift, _ = message
        away = pairs[0] if lent else 0
        if not away and not shift:
            return cut
        route = [(c * seg + s, (c - away) % chan * seg + (s + shift) % seg) for c in range(chan) for s in range(seg)]
        return lax.ppermute(cut, ("chan", "seg"), route)

    windows, powers, done = {}, {}, {}
    for message, cut in zip(plan, cuts):
        pairs, lent, shift, powered = message
        earlier = [done[m] for m in waits_for(message, seg)]
        if earlier:
            cut, *_ = lax.optimization_barrier((cut, *earlier))
        array = done[message] = delivered(message, cut)
        for i, pair in enumerate(pairs):
            windows[pair, lent, shift] = array, i * bins
            if powered:
                powers[pair, lent, shift] = array
    scale = 1.0 / (segs * 0.375 * length) / LIFT**2
    shape = (1, PAIRS, 2, bins, width, width)
    my_power = [powers[0, False, k] for k in range(seg)]
    out = None
    for pair in range(PAIRS):
        mine = [windows[pair, False, k] for k in range(seg)]
        theirs = [windows[pair, True, k] for k in range(seg)] if pair else mine
        their_power = [powers[pair, True, k] for k in range(seg)] if pair else my_power
        out = cross(pair, segs * length, scale, sched, mine, theirs, my_power, their_power, shape, out)
    return out


def solution(mesh):
    in_specs = (P("seg", None, "chan"), P(), P("chan", None))
    out_specs = P("chan", None, None, "seg", None, None)
    return jax.shard_map(body, mesh=mesh, in_specs=in_specs, out_specs=out_specs, check_vma=False)
```

```python
import functools

import jax
import jax.numpy as jnp
import ml_dtypes
import numpy as np
from jax import lax
from jax.experimental import pallas as pl
from jax.experimental.pallas import tpu as pltpu
from jax.sharding import PartitionSpec as P

NB = 256
BW = 64
PAIRS = 4
LANES = 128
LIFT = 1024.0
CROSS_VMEM = 24 << 20
GROUPS = ((0,), (1,), (2, 3))


def dft_table(nbins, length):
    freq = np.arange(nbins)[:, None]
    sample = np.arange(length)[None, :]
    phase = (freq * sample % length) * (2.0 * np.pi / length)
    window = 0.5 - 0.5 * np.cos(sample * (2.0 * np.pi / length))
    table = np.concatenate([window * np.cos(phase), -window * np.sin(phase)])
    return (table.astype(np.float32).astype(ml_dtypes.bfloat16).astype(np.float32) * LIFT).astype(ml_dtypes.bfloat16)


def row_table(table):
    nbins, length = table.shape[0] // 2, table.shape[1]
    rows = table.astype(np.float32).reshape(2, nbins, length // LANES, LANES).transpose(0, 2, 1, 3)
    return np.pad(rows, ((0, 0), (0, 0), (0, 8), (0, 0)))


def message_plan(seg):
    away = range(1, seg)
    first = [((0, 1), False, k, True) for k in away]
    first += [((1,), True, k, True) for k in away]
    plan = [((pair,), True, 0, True) for pair in range(1, PAIRS)]
    plan += [((2, 3), False, k, False) for k in away]
    plan += [((pair,), True, k, True) for pair in (2, 3) for k in away]
    return first, plan + [(tuple(range(PAIRS)), False, 0, True)]


def comes_after(message):
    pairs, lent, shift, _ = message
    return 0 if lent and shift and pairs[0] > 1 else None


def split3(x):
    high = x.astype(jnp.bfloat16)
    rest = x - high.astype(jnp.float32)
    mid = rest.astype(jnp.bfloat16)
    low = (rest - mid.astype(jnp.float32)).astype(jnp.bfloat16)
    return high, mid, low


def first_bin(band_ref, pair, lent, shift, seg):
    block, seat, chan = lax.axis_index("chan"), lax.axis_index("seg"), band_ref.shape[1]
    user = lax.rem(block + (chan - pair), chan) if lent else block
    return band_ref[pair, user] + lax.rem(seat + shift, seg) * (BW // seg)


def power_tile(power, rows):
    width = power.shape[1]
    parts = split3(jnp.sum(power, axis=0, keepdims=True))
    row = lax.broadcasted_iota(jnp.int32, (rows, width), 0)
    packed = jnp.zeros((rows, width), jnp.float32)
    for i, part in enumerate(parts):
        packed = jnp.where(row == i, part.astype(jnp.float32), packed)
    return packed.astype(jnp.bfloat16)


def early_kernel(plan, seg, band_ref, rows_hbm, signal_hbm, *refs):
    n = len(plan)
    outs, (rows_held, signal, raw, cut, row_sem, signal_sem, out_sem) = refs[:n], refs[n:]
    segs, _, width = signal.shape
    rows, bins = 2 * segs, BW // seg
    windows = [first_bin(band_ref, pair, lent, shift, seg) for pairs, lent, shift, _ in plan for pair in pairs]
    row_copies = []
    for w, start in enumerate(windows):
        aligned = pl.multiple_of(start // 8 * 8, 8)
        row_copies.append(pltpu.make_async_copy(rows_hbm.at[:, :, pl.ds(aligned, bins + 8), :], rows_held.at[w], row_sem.at[w]))
    signal_copy = pltpu.make_async_copy(signal_hbm, signal, signal_sem)
    for copy in row_copies:
        copy.start()
    signal_copy.start()
    for copy in row_copies:
        copy.wait()
    pieces = []
    for w, start in enumerate(windows):
        for r in range(2):
            chunks = [rows_held[w, r, k, pl.ds(lax.rem(start, 8), bins), :] for k in range(rows_held.shape[2])]
            pieces.append(jnp.concatenate(chunks, axis=1))
    table = jnp.concatenate(pieces, axis=0).astype(jnp.bfloat16)
    signal_copy.wait()
    power = jnp.zeros((8, width), jnp.float32)
    for s in range(segs):
        spectrum = jnp.dot(table, signal[s], preferred_element_type=jnp.float32)
        for w in range(len(windows)):
            for r in range(2):
                at = (2 * w + r) * bins
                for h in range(width // LANES):
                    raw[h, pl.ds(w * bins * rows + r * segs + s, bins, stride=rows), :] = spectrum[at : at + bins, h * LANES : (h + 1) * LANES]
        x = signal[s].astype(jnp.float32)
        power = power + jnp.sum((x * x).reshape(-1, 8, width), axis=0)
    total = len(windows) * bins
    cut[total] = power_tile(power, rows)
    for h in range(width // LANES):
        cut[:total, :, h * LANES : (h + 1) * LANES] = raw[h].reshape(total, rows, LANES).astype(jnp.bfloat16)
    copies, at = [], 0
    for (pairs, _, _, _), out in zip(plan, outs):
        size = len(pairs) * bins
        copies.append(pltpu.make_async_copy(cut.at[pl.ds(at, size)], out.at[pl.ds(0, size)], out_sem.at[len(copies)]))
        copies.append(pltpu.make_async_copy(cut.at[pl.ds(total, 1)], out.at[pl.ds(size, 1)], out_sem.at[len(copies)]))
        at += size
    for copy in copies:
        copy.start()
    for copy in copies:
        copy.wait()


def early_spectra(plan, seg, band, rows_table, signal):
    segs, length, width = signal.shape
    rows, bins = 2 * segs, BW // seg
    n = sum(len(m[0]) for m in plan)
    anywhere = pl.BlockSpec(memory_space=pl.ANY)
    return pl.pallas_call(
        functools.partial(early_kernel, plan, seg),
        in_specs=[pl.BlockSpec(memory_space=pltpu.SMEM), anywhere, anywhere],
        out_specs=[anywhere] * len(plan),
        out_shape=[message_shape(m, bins, rows, width) for m in plan],
        scratch_shapes=[
            pltpu.VMEM((n, 2, length // LANES, bins + 8, LANES), jnp.float32),
            pltpu.VMEM(signal.shape, jnp.bfloat16),
            pltpu.VMEM((width // LANES, n * bins * rows, LANES), jnp.float32),
            pltpu.VMEM((n * bins + 1, rows, width), jnp.bfloat16),
            pltpu.SemaphoreType.DMA((n,)),
            pltpu.SemaphoreType.DMA,
            pltpu.SemaphoreType.DMA((2 * len(plan),)),
        ],
        compiler_params=pltpu.CompilerParams(vmem_limit_bytes=56 << 20),
    )(band, rows_table, signal)


def spectra_kernel(plan, seg, band_ref, table_hbm, signal_hbm, early_hbm, *refs):
    n = len(plan)
    outs, (table, signal, raw, spectra, table_sem, signal_sem, power_sem, out_sem) = refs[:n], refs[n:]
    segs, _, width = signal.shape
    nbins = table.shape[0] // 2
    rows = 2 * segs
    bins = BW // seg
    table_copy = pltpu.make_async_copy(table_hbm, table, table_sem)
    signal_copy = pltpu.make_async_copy(signal_hbm, signal, signal_sem)
    power_copy = pltpu.make_async_copy(early_hbm.at[pl.ds(early_hbm.shape[0] - 1, 1)], spectra.at[pl.ds(nbins, 1)], power_sem)
    table_copy.start()
    power_copy.start()
    signal_copy.start()
    table_copy.wait()
    power_copy.wait()
    signal_copy.wait()
    for s in range(segs):
        spectrum = jnp.dot(table[...], signal[s], preferred_element_type=jnp.float32)
        for r in range(2):
            for h in range(width // LANES):
                raw[h, pl.ds(r * segs + s, nbins, stride=rows), :] = spectrum[r * nbins : (r + 1) * nbins, h * LANES : (h + 1) * LANES]
    for h in range(width // LANES):
        spectra[:nbins, :, h * LANES : (h + 1) * LANES] = raw[h].reshape(nbins, rows, LANES).astype(jnp.bfloat16)
    copies = []
    for (pairs, lent, shift, powered), out in zip(plan, outs):
        pieces = [(first_bin(band_ref, pair, lent, shift, seg), bins) for pair in pairs] + [(nbins, 1)] * powered
        for i, (start, size) in enumerate(pieces):
            copies.append(pltpu.make_async_copy(spectra.at[pl.ds(start, size)], out.at[pl.ds(i * bins, size)], out_sem.at[len(copies)]))
    for copy in copies:
        copy.start()
    for copy in copies:
        copy.wait()


def message_shape(message, bins, rows, width):
    pairs, _, _, powered = message
    return jax.ShapeDtypeStruct((len(pairs) * bins + powered, rows, width), jnp.bfloat16)


def make_spectra(plan, seg, band, table, signal, early):
    segs, length, width = signal.shape
    rows, bins, n, nbins = 2 * segs, BW // seg, len(plan), table.shape[0] // 2
    anywhere = pl.BlockSpec(memory_space=pl.ANY)
    return pl.pallas_call(
        functools.partial(spectra_kernel, plan, seg),
        in_specs=[pl.BlockSpec(memory_space=pltpu.SMEM)] + [anywhere] * 3,
        out_specs=[anywhere] * n,
        out_shape=[message_shape(m, bins, rows, width) for m in plan],
        scratch_shapes=[
            pltpu.VMEM(table.shape, jnp.bfloat16),
            pltpu.VMEM(signal.shape, jnp.bfloat16),
            pltpu.VMEM((width // LANES, nbins * rows, LANES), jnp.float32),
            pltpu.VMEM((nbins + 1, rows, width), jnp.bfloat16),
            pltpu.SemaphoreType.DMA,
            pltpu.SemaphoreType.DMA,
            pltpu.SemaphoreType.DMA,
            pltpu.SemaphoreType.DMA((sum(len(m[0]) + m[3] for m in plan),)),
        ],
        compiler_params=pltpu.CompilerParams(vmem_limit_bytes=56 << 20),
        cost_estimate=pl.CostEstimate(flops=2 * table.size * segs * width, bytes_accessed=32 << 20, transcendentals=0),
    )(band, table, signal, early)


def turned(y):
    half = y.shape[0] // 2
    return jnp.concatenate([-y[half:], y[:half]], axis=0)


def inv_rms_of(tiles, samples):
    power = 0.0
    for tile in tiles:
        t = tile.astype(jnp.float32)
        power = power + (t[0:1] + t[1:2] + t[2:3])
    return lax.rsqrt(power / samples + 1e-06)


def cross_kernel(pairs, loads, samples, scale, sched_hbm, *refs):
    *arrays, out, sched_ref, held, ring, weight, sched_sem, in_sem, out_sem = refs
    sched_copy = pltpu.make_async_copy(sched_hbm, sched_ref, sched_sem)
    sched_copy.start()
    width = held.shape[-1]
    _, depth, _, chunk = ring.shape[:4]
    bins = out.shape[3]
    steps = bins // chunk
    in_copies, out_copies, zero_copies = {}, [], []
    for load in loads:
        for array, first, size, slot in sum(load, []):
            if slot not in in_copies:
                in_copies[slot] = pltpu.make_async_copy(arrays[array].at[pl.ds(first, size)], held.at[slot, pl.ds(0, size)], in_sem.at[slot])
    for i, pair in enumerate(pairs):
        for source, copies in ((lambda c: c % depth, out_copies), (lambda c: 0, zero_copies)):
            copies.append(
                [
                    pltpu.make_async_copy(ring.at[i, source(c)], out.at[0, pair, :, pl.ds(c * chunk, chunk)], out_sem.at[i, c])
                    for c in range(steps)
                ]
            )
    for copy in in_copies.values():
        copy.start()
    sched_copy.wait()
    waited = set()
    for i, pair in enumerate(pairs):
        x_loads, y_loads, x_power, y_power = ([slot for _, _, _, slot in part] for part in loads[i])
        for slot in x_loads + y_loads + x_power + y_power:
            if slot not in waited:
                in_copies[slot].wait()
                waited.add(slot)
        live = sched_ref[0, pair]

        @pl.when(live == 0)
        def _(i=i):
            ring[i, 0] = jnp.zeros(ring.shape[2:], ring.dtype)
            for c, copy in enumerate(zero_copies[i]):
                copy.start()
            for copy in zero_copies[i][: max(steps - depth, 0)]:
                copy.wait()

        @pl.when(live != 0)
        def _(i=i, x_loads=x_loads, y_loads=y_loads, x_power=x_power, y_power=y_power):
            by_row = jnp.broadcast_to(inv_rms_of([held[k, 0] for k in x_power], samples) * scale, (width, width)).T
            weight[...] = by_row * inv_rms_of([held[k, 0] for k in y_power], samples)
            for c in range(steps):
                if c >= depth:
                    out_copies[i][c - depth].wait()
                for f in range(c * chunk, (c + 1) * chunk):
                    x = jnp.concatenate([held[k, f] for k in x_loads], axis=0)
                    y = jnp.concatenate([held[k, f] for k in y_loads], axis=0)
                    y_turned = jnp.concatenate([turned(held[k, f]) for k in y_loads], axis=0)
                    partner = jnp.concatenate([y, y_turned], axis=1)
                    product = lax.dot_general(x, partner, (((0,), (0,)), ((), ())), preferred_element_type=jnp.float32)
                    for r in range(2):
                        part = product[:, r * width : (r + 1) * width] * weight[...]
                        ring[i, c % depth, r, f - c * chunk] = part.astype(ring.dtype)
                out_copies[i][c].start()

    for copies in out_copies:
        for copy in copies[max(steps - depth, 0) :]:
            copy.wait()


def cross(pairs, seg, samples, scale, sched, windows, powers, shape, out):
    bins, width = shape[3], shape[4]
    chunk = min(8, bins)
    arrays, slots, loads = [], {}, []

    def load(array, first, size):
        known = [k for k, other in enumerate(arrays) if other is array]
        if not known:
            arrays.append(array)
        where = (known[0] if known else len(arrays) - 1, first, size)
        return (*where, slots.setdefault(where, len(slots)))

    for pair in pairs:
        x, y = ([load(*windows[pair, lent, k], bins) for k in range(seg)] for lent in (False, pair > 0))
        tiles = [[powers[p, lent, k] for k in range(seg)] for p, lent in ((0, False), (pair, pair > 0))]
        loads.append([x, y] + [[load(array, array.shape[0] - 1, 1) for array in part] for part in tiles])
    rows, kept = arrays[0].shape[1], windows[0, False, 0][0]
    anywhere, in_hbm = pl.BlockSpec(memory_space=pl.ANY), pl.BlockSpec(memory_space=pltpu.HBM)
    operands = [sched, *arrays]
    aliases = {}
    if out is not None:
        aliases = {len(operands): 0}
        operands.append(out)
    kernel = functools.partial(cross_kernel, pairs, loads, samples, scale)
    if out is not None:
        kernel = functools.partial(drop_ref, len(operands) - 1, kernel)
    return pl.pallas_call(
        kernel,
        in_specs=[in_hbm if a is sched or a is kept else anywhere for a in operands],
        out_specs=anywhere,
        scratch_shapes=[
            pltpu.SMEM(sched.shape, jnp.int32),
            pltpu.VMEM((len(slots), bins, rows, width), jnp.bfloat16),
            pltpu.VMEM((len(pairs), 3, 2, chunk, width, width), jnp.bfloat16),
            pltpu.VMEM((width, width), jnp.float32),
            pltpu.SemaphoreType.DMA,
            pltpu.SemaphoreType.DMA((len(slots),)),
            pltpu.SemaphoreType.DMA((len(pairs), bins // chunk)),
        ],
        out_shape=jax.ShapeDtypeStruct(shape, jnp.bfloat16),
        input_output_aliases=aliases,
        compiler_params=pltpu.CompilerParams(vmem_limit_bytes=CROSS_VMEM),
        cost_estimate=pl.CostEstimate(
            flops=4 * len(pairs) * bins * seg * rows * width * width,
            bytes_accessed=4 * len(pairs) * bins * width * width,
            transcendentals=0,
        ),
    )(*operands)


def drop_ref(k, kernel, *refs):
    return kernel(*refs[:k], *refs[k + 1 :])


def body(signal, band, sched):
    seg_dev, length, width = signal.shape
    seg, chan = lax.axis_size("seg"), lax.axis_size("chan")
    segs = seg_dev * seg
    bins = BW // seg
    first, plan = message_plan(seg)
    table = dft_table(NB, length)
    cuts = early_spectra(first, seg, band.T, jnp.asarray(row_table(table)), signal)
    cuts += make_spectra(plan, seg, band.T, jnp.asarray(table), signal, cuts[0])

    def delivered(message, cut):
        pairs, lent, shift, _ = message
        away = pairs[0] if lent else 0
        if not away and not shift:
            return cut
        route = [(c * seg + s, (c - away) % chan * seg + (s + shift) % seg) for c in range(chan) for s in range(seg)]
        return lax.ppermute(cut, ("chan", "seg"), route)

    windows, powers = {}, {}
    scale = 1.0 / (segs * 0.375 * length) / LIFT**2
    shape = (1, PAIRS, 2, bins, width, width)
    out = None

    def deliver(message, cut, out=None):
        if out is not None:
            cut, out = lax.optimization_barrier((cut, out))
        pairs, lent, shift, powered = message
        array = delivered(message, cut)
        for i, pair in enumerate(pairs):
            windows[pair, lent, shift] = array, i * bins
            if powered:
                powers[pair, lent, shift] = array
        return out

    cuts = dict(zip(first + plan, cuts))
    for message, cut in cuts.items():
        if comes_after(message) is None:
            deliver(message, cut)
    for pairs in GROUPS:
        out = cross(pairs, seg, segs * length, scale, sched, windows, powers, shape, out)
        for message, cut in cuts.items():
            if comes_after(message) == pairs[-1]:
                out = deliver(message, cut, out)
    return out


def solution(mesh):
    in_specs = (P("seg", None, "chan"), P(), P("chan", None))
    out_specs = P("chan", None, None, "seg", None, None)
    return jax.shard_map(body, mesh=mesh, in_specs=in_specs, out_specs=out_specs, check_vma=False)
```

```python
import functools

import jax
import jax.numpy as jnp
import ml_dtypes
import numpy as np
from jax import lax
from jax.experimental import pallas as pl
from jax.experimental.pallas import tpu as pltpu
from jax.sharding import PartitionSpec as P

NB = 256
BW = 64
PAIRS = 4
LANES = 128
LIFT = 1024.0
CROSS_VMEM = 24 << 20
GROUPS = ((0,), (1,), (2, 3))
CHUNK = 8


def dft_table(nbins, length):
    freq = np.arange(nbins)[:, None]
    sample = np.arange(length)[None, :]
    phase = (freq * sample % length) * (2.0 * np.pi / length)
    window = 0.5 - 0.5 * np.cos(sample * (2.0 * np.pi / length))
    table = np.concatenate([window * np.cos(phase), -window * np.sin(phase)])
    return (table.astype(np.float32).astype(ml_dtypes.bfloat16).astype(np.float32) * LIFT).astype(ml_dtypes.bfloat16)


def row_table(table):
    nbins, length = table.shape[0] // 2, table.shape[1]
    rows = table.astype(np.float32).reshape(2, nbins, length // LANES, LANES).transpose(0, 2, 1, 3)
    return np.pad(rows, ((0, 0), (0, 0), (0, 8), (0, 0)))


def message_plan(seg):
    away = range(1, seg)
    first = [((0, 1), False, k, True) for k in away]
    first += [((1,), True, k, True) for k in away]
    plan = [((pair,), True, 0, True) for pair in range(1, PAIRS)]
    plan += [((2, 3), False, k, False) for k in away]
    plan += [((pair,), True, k, True) for pair in (2, 3) for k in away]
    return first, plan + [(tuple(range(PAIRS)), False, 0, True)]


def comes_after(message):
    pairs, lent, shift, _ = message
    return 0 if lent and shift and pairs[0] > 1 else None


def split3(x):
    high = x.astype(jnp.bfloat16)
    rest = x - high.astype(jnp.float32)
    mid = rest.astype(jnp.bfloat16)
    low = (rest - mid.astype(jnp.float32)).astype(jnp.bfloat16)
    return high, mid, low


def first_bin(band_ref, pair, lent, shift, seg):
    block, seat, chan = lax.axis_index("chan"), lax.axis_index("seg"), band_ref.shape[1]
    user = lax.rem(block + (chan - pair), chan) if lent else block
    return band_ref[pair, user] + lax.rem(seat + shift, seg) * (BW // seg)


def power_tile(power, rows):
    width = power.shape[1]
    parts = split3(jnp.sum(power, axis=0, keepdims=True))
    row = lax.broadcasted_iota(jnp.int32, (rows, width), 0)
    packed = jnp.zeros((rows, width), jnp.float32)
    for i, part in enumerate(parts):
        packed = jnp.where(row == i, part.astype(jnp.float32), packed)
    return packed.astype(jnp.bfloat16)


def early_kernel(plan, seg, band_ref, rows_hbm, signal_hbm, *refs):
    n = len(plan)
    outs, (rows_held, signal, raw, cut, row_sem, signal_sem, out_sem) = refs[:n], refs[n:]
    segs, _, width = signal.shape
    rows, bins = 2 * segs, BW // seg
    windows = [first_bin(band_ref, pair, lent, shift, seg) for pairs, lent, shift, _ in plan for pair in pairs]
    row_copies = []
    for w, start in enumerate(windows):
        aligned = pl.multiple_of(start // 8 * 8, 8)
        row_copies.append(pltpu.make_async_copy(rows_hbm.at[:, :, pl.ds(aligned, bins + 8), :], rows_held.at[w], row_sem.at[w]))
    signal_copies = [pltpu.make_async_copy(signal_hbm.at[s], signal.at[s], signal_sem.at[s]) for s in range(segs)]
    for copy in row_copies:
        copy.start()
    for copy in signal_copies:
        copy.start()
    for copy in row_copies:
        copy.wait()
    pieces = []
    for w, start in enumerate(windows):
        for r in range(2):
            chunks = [rows_held[w, r, k, pl.ds(lax.rem(start, 8), bins), :] for k in range(rows_held.shape[2])]
            pieces.append(jnp.concatenate(chunks, axis=1))
    table = jnp.concatenate(pieces, axis=0).astype(jnp.bfloat16)
    for copy in signal_copies:
        copy.wait()
    power = jnp.zeros((8, width), jnp.float32)
    for s in range(segs):
        spectrum = jnp.dot(table, signal[s], preferred_element_type=jnp.float32)
        for w in range(len(windows)):
            for r in range(2):
                at = (2 * w + r) * bins
                for h in range(width // LANES):
                    raw[h, pl.ds(w * bins * rows + r * segs + s, bins, stride=rows), :] = spectrum[at : at + bins, h * LANES : (h + 1) * LANES]
        x = signal[s].astype(jnp.float32)
        power = power + jnp.sum((x * x).reshape(-1, 8, width), axis=0)
    total = len(windows) * bins
    cut[total] = power_tile(power, rows)
    for h in range(width // LANES):
        cut[:total, :, h * LANES : (h + 1) * LANES] = raw[h, : total * rows].reshape(total, rows, LANES).astype(jnp.bfloat16)
    copies, at = [], 0
    for (pairs, _, _, _), out in zip(plan, outs):
        size = len(pairs) * bins
        copies.append(pltpu.make_async_copy(cut.at[pl.ds(at, size)], out.at[pl.ds(0, size)], out_sem.at[len(copies)]))
        copies.append(pltpu.make_async_copy(cut.at[pl.ds(total, 1)], out.at[pl.ds(size, 1)], out_sem.at[len(copies)]))
        at += size
    for copy in copies:
        copy.start()
    for copy in copies:
        copy.wait()


def early_spectra(plan, seg, band, rows_table, signal):
    segs, length, width = signal.shape
    rows, bins = 2 * segs, BW // seg
    n = sum(len(m[0]) for m in plan)
    anywhere = pl.BlockSpec(memory_space=pl.ANY)
    return pl.pallas_call(
        functools.partial(early_kernel, plan, seg),
        in_specs=[pl.BlockSpec(memory_space=pltpu.SMEM), anywhere, anywhere],
        out_specs=[anywhere] * len(plan),
        out_shape=[message_shape(m, bins, rows, width) for m in plan],
        scratch_shapes=[
            pltpu.VMEM((n, 2, length // LANES, bins + 8, LANES), jnp.float32),
            pltpu.VMEM(signal.shape, jnp.bfloat16),
            pltpu.VMEM((width // LANES, (n * bins + 1) * rows, LANES), jnp.float32),
            pltpu.VMEM((n * bins + 1, rows, width), jnp.bfloat16),
            pltpu.SemaphoreType.DMA((n,)),
            pltpu.SemaphoreType.DMA((segs,)),
            pltpu.SemaphoreType.DMA((2 * len(plan),)),
        ],
        compiler_params=pltpu.CompilerParams(vmem_limit_bytes=56 << 20),
    )(band, rows_table, signal)


def spectra_kernel(plan, seg, band_ref, table_hbm, signal_hbm, early_hbm, *refs):
    n = len(plan)
    outs, (table, signal, raw, spectra, table_sem, signal_sem, power_sem, out_sem) = refs[:n], refs[n:]
    segs, _, width = signal.shape
    nbins = table.shape[0] // 2
    rows = 2 * segs
    bins = BW // seg
    table_copy = pltpu.make_async_copy(table_hbm, table, table_sem)
    signal_copies = [pltpu.make_async_copy(signal_hbm.at[s], signal.at[s], signal_sem.at[s]) for s in range(segs)]
    power_copy = pltpu.make_async_copy(early_hbm.at[pl.ds(early_hbm.shape[0] - 1, 1)], spectra.at[pl.ds(nbins, 1)], power_sem)
    table_copy.start()
    power_copy.start()
    for copy in signal_copies:
        copy.start()
    table_copy.wait()
    power_copy.wait()
    for copy in signal_copies:
        copy.wait()
    for s in range(segs):
        spectrum = jnp.dot(table[...], signal[s], preferred_element_type=jnp.float32)
        for r in range(2):
            for h in range(width // LANES):
                raw[h, pl.ds(r * segs + s, nbins, stride=rows), :] = spectrum[r * nbins : (r + 1) * nbins, h * LANES : (h + 1) * LANES]
    for h in range(width // LANES):
        spectra[:nbins, :, h * LANES : (h + 1) * LANES] = raw[h, : nbins * rows].reshape(nbins, rows, LANES).astype(jnp.bfloat16)
    copies = []
    for (pairs, lent, shift, powered), out in zip(plan, outs):
        pieces = [(first_bin(band_ref, pair, lent, shift, seg), bins) for pair in pairs] + [(nbins, 1)] * powered
        for i, (start, size) in enumerate(pieces):
            copies.append(pltpu.make_async_copy(spectra.at[pl.ds(start, size)], out.at[pl.ds(i * bins, size)], out_sem.at[len(copies)]))
    for copy in copies:
        copy.start()
    for copy in copies:
        copy.wait()


def message_shape(message, bins, rows, width):
    pairs, _, _, powered = message
    return jax.ShapeDtypeStruct((len(pairs) * bins + powered, rows, width), jnp.bfloat16)


def make_spectra(plan, seg, band, table, signal, early):
    segs, length, width = signal.shape
    rows, bins, n, nbins = 2 * segs, BW // seg, len(plan), table.shape[0] // 2
    anywhere = pl.BlockSpec(memory_space=pl.ANY)
    return pl.pallas_call(
        functools.partial(spectra_kernel, plan, seg),
        in_specs=[pl.BlockSpec(memory_space=pltpu.SMEM)] + [anywhere] * 3,
        out_specs=[anywhere] * n,
        out_shape=[message_shape(m, bins, rows, width) for m in plan],
        scratch_shapes=[
            pltpu.VMEM(table.shape, jnp.bfloat16),
            pltpu.VMEM(signal.shape, jnp.bfloat16),
            pltpu.VMEM((width // LANES, (nbins + 1) * rows, LANES), jnp.float32),
            pltpu.VMEM((nbins + 1, rows, width), jnp.bfloat16),
            pltpu.SemaphoreType.DMA,
            pltpu.SemaphoreType.DMA((segs,)),
            pltpu.SemaphoreType.DMA,
            pltpu.SemaphoreType.DMA((sum(len(m[0]) + m[3] for m in plan),)),
        ],
        compiler_params=pltpu.CompilerParams(vmem_limit_bytes=56 << 20),
        cost_estimate=pl.CostEstimate(flops=2 * table.size * segs * width, bytes_accessed=32 << 20, transcendentals=0),
    )(band, table, signal, early)


def turned(y):
    half = y.shape[0] // 2
    return jnp.concatenate([-y[half:], y[:half]], axis=0)


def inv_rms_of(tiles, samples):
    power = 0.0
    for tile in tiles:
        t = tile.astype(jnp.float32)
        power = power + (t[0:1] + t[1:2] + t[2:3])
    return lax.rsqrt(power / samples + 1e-06)


def chunks_of(bins, lead, trail):
    sizes = [min(CHUNK, bins - f) for f in range(0, bins, CHUNK)]
    if lead and sizes[0] > 2:
        sizes[:1] = [2, sizes[0] - 2]
    if trail and sizes[-1] > 2:
        sizes[-1:] = [sizes[-1] - sizes[-1] // 2, sizes[-1] // 2]
    return [(sum(sizes[:c]), size) for c, size in enumerate(sizes)]


def cross_kernel(pairs, loads, samples, scale, sched_hbm, *refs):
    *arrays, out, sched_ref, held, ring, weight, sched_sem, in_sem, out_sem = refs
    sched_copy = pltpu.make_async_copy(sched_hbm, sched_ref, sched_sem)
    sched_copy.start()
    width = held.shape[-1]
    depth = ring.shape[1]
    chunks = [chunks_of(out.shape[3], i == 0, i == len(pairs) - 1) for i in range(len(pairs))]
    in_copies, out_copies, zero_copies = {}, [], []
    for load in loads:
        for array, first, size, slot in sum(load, []):
            if slot not in in_copies:
                in_copies[slot] = pltpu.make_async_copy(arrays[array].at[pl.ds(first, size)], held.at[slot, pl.ds(0, size)], in_sem.at[slot])
    for i, pair in enumerate(pairs):
        for slots, copies in ((depth, out_copies), (1, zero_copies)):
            copies.append(
                [
                    pltpu.make_async_copy(
                        ring.at[i, c % slots, :, pl.ds(0, size)], out.at[0, pair, :, pl.ds(first, size)], out_sem.at[i, c]
                    )
                    for c, (first, size) in enumerate(chunks[i])
                ]
            )
    fresh, known = [], set()
    for load in loads:
        fresh.append([slot for *_, slot in sum(load, []) if slot not in known])
        fresh[-1] = list(dict.fromkeys(fresh[-1]))
        known.update(fresh[-1])
    for slot in fresh[0]:
        in_copies[slot].start()
    sched_copy.wait()
    for i, pair in enumerate(pairs):
        x_loads, y_loads, x_power, y_power = ([slot for _, _, _, slot in part] for part in loads[i])
        for slot in fresh[i]:
            in_copies[slot].wait()
        for slot in fresh[i + 1] if i + 1 < len(pairs) else []:
            in_copies[slot].start()
        live = sched_ref[0, pair]

        @pl.when(live == 0)
        def _(i=i):
            ring[i, 0] = jnp.zeros(ring.shape[2:], ring.dtype)
            for c, copy in enumerate(zero_copies[i]):
                copy.start()
            for copy in zero_copies[i][:-depth]:
                copy.wait()

        @pl.when(live != 0)
        def _(i=i, x_loads=x_loads, y_loads=y_loads, x_power=x_power, y_power=y_power):
            by_row = jnp.broadcast_to(inv_rms_of([held[k, 0] for k in x_power], samples) * scale, (width, width)).T
            weight[...] = by_row * inv_rms_of([held[k, 0] for k in y_power], samples)
            for c, (first, size) in enumerate(chunks[i]):
                if c >= depth:
                    out_copies[i][c - depth].wait()
                for f in range(first, first + size):
                    x = jnp.concatenate([held[k, f] for k in x_loads], axis=0)
                    y = jnp.concatenate([held[k, f] for k in y_loads], axis=0)
                    y_turned = jnp.concatenate([turned(held[k, f]) for k in y_loads], axis=0)
                    partner = jnp.concatenate([y, y_turned], axis=1)
                    product = lax.dot_general(x, partner, (((0,), (0,)), ((), ())), preferred_element_type=jnp.float32)
                    for r in range(2):
                        part = product[:, r * width : (r + 1) * width] * weight[...]
                        ring[i, c % depth, r, f - first] = part.astype(ring.dtype)
                out_copies[i][c].start()

    for copies in out_copies:
        for copy in copies[-depth:]:
            copy.wait()


def cross(pairs, seg, samples, scale, sched, windows, powers, shape, out):
    bins, width = shape[3], shape[4]
    arrays, slots, loads = [], {}, []

    def load(array, first, size):
        known = [k for k, other in enumerate(arrays) if other is array]
        if not known:
            arrays.append(array)
        where = (known[0] if known else len(arrays) - 1, first, size)
        return (*where, slots.setdefault(where, len(slots)))

    for pair in pairs:
        x, y = ([load(*windows[pair, lent, k], bins) for k in range(seg)] for lent in (False, pair > 0))
        tiles = [[powers[p, lent, k] for k in range(seg)] for p, lent in ((0, False), (pair, pair > 0))]
        loads.append([x, y] + [[load(array, array.shape[0] - 1, 1) for array in part] for part in tiles])
    rows, kept = arrays[0].shape[1], windows[0, False, 0][0]
    anywhere, in_hbm = pl.BlockSpec(memory_space=pl.ANY), pl.BlockSpec(memory_space=pltpu.HBM)
    operands = [sched, *arrays]
    aliases = {}
    if out is not None:
        aliases = {len(operands): 0}
        operands.append(out)
    kernel = functools.partial(cross_kernel, pairs, loads, samples, scale)
    if out is not None:
        kernel = functools.partial(drop_ref, len(operands) - 1, kernel)
    return pl.pallas_call(
        kernel,
        in_specs=[in_hbm if a is sched or a is kept else anywhere for a in operands],
        out_specs=anywhere,
        scratch_shapes=[
            pltpu.SMEM(sched.shape, jnp.int32),
            pltpu.VMEM((len(slots), bins, rows, width), jnp.bfloat16),
            pltpu.VMEM((len(pairs), 3, 2, min(CHUNK, bins), width, width), jnp.bfloat16),
            pltpu.VMEM((width, width), jnp.float32),
            pltpu.SemaphoreType.DMA,
            pltpu.SemaphoreType.DMA((len(slots),)),
            pltpu.SemaphoreType.DMA((len(pairs), bins // min(CHUNK, bins) + 2)),
        ],
        out_shape=jax.ShapeDtypeStruct(shape, jnp.bfloat16),
        input_output_aliases=aliases,
        compiler_params=pltpu.CompilerParams(vmem_limit_bytes=CROSS_VMEM),
        cost_estimate=pl.CostEstimate(
            flops=4 * len(pairs) * bins * seg * rows * width * width,
            bytes_accessed=4 * len(pairs) * bins * width * width,
            transcendentals=0,
        ),
    )(*operands)


def drop_ref(k, kernel, *refs):
    return kernel(*refs[:k], *refs[k + 1 :])


def body(signal, band, sched):
    seg_dev, length, width = signal.shape
    seg, chan = lax.axis_size("seg"), lax.axis_size("chan")
    segs = seg_dev * seg
    bins = BW // seg
    first, plan = message_plan(seg)
    table = dft_table(NB, length)
    cuts = early_spectra(first, seg, band.T, jnp.asarray(row_table(table)), signal)
    cuts += make_spectra(plan, seg, band.T, jnp.asarray(table), signal, cuts[0])

    def delivered(message, cut):
        pairs, lent, shift, _ = message
        away = pairs[0] if lent else 0
        if not away and not shift:
            return cut
        route = [(c * seg + s, (c - away) % chan * seg + (s + shift) % seg) for c in range(chan) for s in range(seg)]
        return lax.ppermute(cut, ("chan", "seg"), route)

    windows, powers = {}, {}
    scale = 1.0 / (segs * 0.375 * length) / LIFT**2
    shape = (1, PAIRS, 2, bins, width, width)
    out = None

    def deliver(message, cut, out=None):
        if out is not None:
            cut, out = lax.optimization_barrier((cut, out))
        pairs, lent, shift, powered = message
        array = delivered(message, cut)
        for i, pair in enumerate(pairs):
            windows[pair, lent, shift] = array, i * bins
            if powered:
                powers[pair, lent, shift] = array
        return out

    cuts = dict(zip(first + plan, cuts))
    for message, cut in cuts.items():
        if comes_after(message) is None:
            deliver(message, cut)
    for pairs in GROUPS:
        out = cross(pairs, seg, segs * length, scale, sched, windows, powers, shape, out)
        for message, cut in cuts.items():
            if comes_after(message) == pairs[-1]:
                out = deliver(message, cut, out)
    return out


def solution(mesh):
    in_specs = (P("seg", None, "chan"), P(), P("chan", None))
    out_specs = P("chan", None, None, "seg", None, None)
    return jax.shard_map(body, mesh=mesh, in_specs=in_specs, out_specs=out_specs, check_vma=False)
```

```python
import functools

import jax
import jax.numpy as jnp
import ml_dtypes
import numpy as np
from jax import lax
from jax.experimental import pallas as pl
from jax.experimental.pallas import tpu as pltpu
from jax.sharding import PartitionSpec as P

NB = 256
BW = 64
PAIRS = 4
LANES = 128
LIFT = 1024.0
CROSS_VMEM = 24 << 20
GROUPS = ((0,), (1,), (2, 3))
CHUNK = 8


def dft_table(nbins, length):
    freq = np.arange(nbins)[:, None]
    sample = np.arange(length)[None, :]
    phase = (freq * sample % length) * (2.0 * np.pi / length)
    window = 0.5 - 0.5 * np.cos(sample * (2.0 * np.pi / length))
    table = np.concatenate([window * np.cos(phase), -window * np.sin(phase)])
    return (table.astype(np.float32).astype(ml_dtypes.bfloat16).astype(np.float32) * LIFT).astype(ml_dtypes.bfloat16)


def row_table(table):
    nbins, length = table.shape[0] // 2, table.shape[1]
    rows = table.astype(np.float32).reshape(2, nbins, length // LANES, LANES).transpose(0, 2, 1, 3)
    return np.pad(rows, ((0, 0), (0, 0), (0, 8), (0, 0)))


def message_plan(seg):
    away = range(1, seg)
    first = [((0, 1), False, k, True) for k in away]
    first += [((1,), True, k, True) for k in away]
    plan = [((pair,), True, 0, True) for pair in range(1, PAIRS)]
    plan += [((2, 3), False, k, False) for k in away]
    plan += [((pair,), True, k, True) for pair in (2, 3) for k in away]
    return first, plan + [(tuple(range(PAIRS)), False, 0, True)]


def comes_after(message):
    pairs, lent, shift, _ = message
    return 0 if lent and shift and pairs[0] > 1 else None


def split3(x):
    high = x.astype(jnp.bfloat16)
    rest = x - high.astype(jnp.float32)
    mid = rest.astype(jnp.bfloat16)
    low = (rest - mid.astype(jnp.float32)).astype(jnp.bfloat16)
    return high, mid, low


def first_bin(band_ref, pair, lent, shift, seg):
    block, seat, chan = lax.axis_index("chan"), lax.axis_index("seg"), band_ref.shape[1]
    user = lax.rem(block + (chan - pair), chan) if lent else block
    return band_ref[pair, user] + lax.rem(seat + shift, seg) * (BW // seg)


def power_tile(power, rows):
    width = power.shape[1]
    parts = split3(jnp.sum(power, axis=0, keepdims=True))
    row = lax.broadcasted_iota(jnp.int32, (rows, width), 0)
    packed = jnp.zeros((rows, width), jnp.float32)
    for i, part in enumerate(parts):
        packed = jnp.where(row == i, part.astype(jnp.float32), packed)
    return packed.astype(jnp.bfloat16)


def early_kernel(plan, seg, band_ref, rows_hbm, signal_hbm, *refs):
    n = len(plan)
    outs, (rows_held, signal, raw, cut, row_sem, signal_sem, out_sem) = refs[:n], refs[n:]
    segs, _, width = signal.shape
    rows, bins = 2 * segs, BW // seg
    windows = [first_bin(band_ref, pair, lent, shift, seg) for pairs, lent, shift, _ in plan for pair in pairs]
    row_copies = []
    for w, start in enumerate(windows):
        aligned = pl.multiple_of(start // 8 * 8, 8)
        row_copies.append(pltpu.make_async_copy(rows_hbm.at[:, :, pl.ds(aligned, bins + 8), :], rows_held.at[w], row_sem.at[w]))
    signal_copies = [pltpu.make_async_copy(signal_hbm.at[s], signal.at[s], signal_sem.at[s]) for s in range(segs)]
    for copy in row_copies:
        copy.start()
    for copy in signal_copies:
        copy.start()
    for copy in row_copies:
        copy.wait()
    pieces = []
    for w, start in enumerate(windows):
        for r in range(2):
            chunks = [rows_held[w, r, k, pl.ds(lax.rem(start, 8), bins), :] for k in range(rows_held.shape[2])]
            pieces.append(jnp.concatenate(chunks, axis=1))
    table = jnp.concatenate(pieces, axis=0).astype(jnp.bfloat16)
    for copy in signal_copies:
        copy.wait()
    power = jnp.zeros((8, width), jnp.float32)
    for s in range(segs):
        spectrum = jnp.dot(table, signal[s], preferred_element_type=jnp.float32)
        for w in range(len(windows)):
            for r in range(2):
                at = (2 * w + r) * bins
                for h in range(width // LANES):
                    raw[h, pl.ds(w * bins * rows + r * segs + s, bins, stride=rows), :] = spectrum[at : at + bins, h * LANES : (h + 1) * LANES]
        x = signal[s].astype(jnp.float32)
        power = power + jnp.sum((x * x).reshape(-1, 8, width), axis=0)
    total = len(windows) * bins
    cut[total] = power_tile(power, rows)
    for h in range(width // LANES):
        cut[:total, :, h * LANES : (h + 1) * LANES] = raw[h, : total * rows].reshape(total, rows, LANES).astype(jnp.bfloat16)
    copies, at = [], 0
    for (pairs, _, _, _), out in zip(plan, outs):
        size = len(pairs) * bins
        copies.append(pltpu.make_async_copy(cut.at[pl.ds(at, size)], out.at[pl.ds(0, size)], out_sem.at[len(copies)]))
        copies.append(pltpu.make_async_copy(cut.at[pl.ds(total, 1)], out.at[pl.ds(size, 1)], out_sem.at[len(copies)]))
        at += size
    for copy in copies:
        copy.start()
    for copy in copies:
        copy.wait()


def early_spectra(plan, seg, band, rows_table, signal):
    segs, length, width = signal.shape
    rows, bins = 2 * segs, BW // seg
    n = sum(len(m[0]) for m in plan)
    anywhere = pl.BlockSpec(memory_space=pl.ANY)
    return pl.pallas_call(
        functools.partial(early_kernel, plan, seg),
        in_specs=[pl.BlockSpec(memory_space=pltpu.SMEM), anywhere, anywhere],
        out_specs=[anywhere] * len(plan),
        out_shape=[message_shape(m, bins, rows, width) for m in plan],
        scratch_shapes=[
            pltpu.VMEM((n, 2, length // LANES, bins + 8, LANES), jnp.float32),
            pltpu.VMEM(signal.shape, jnp.bfloat16),
            pltpu.VMEM((width // LANES, (n * bins + 1) * rows, LANES), jnp.float32),
            pltpu.VMEM((n * bins + 1, rows, width), jnp.bfloat16),
            pltpu.SemaphoreType.DMA((n,)),
            pltpu.SemaphoreType.DMA((segs,)),
            pltpu.SemaphoreType.DMA((2 * len(plan),)),
        ],
        compiler_params=pltpu.CompilerParams(vmem_limit_bytes=56 << 20),
    )(band, rows_table, signal)


def spectra_kernel(plan, seg, band_ref, table_hbm, signal_hbm, early_hbm, *refs):
    n = len(plan)
    outs, (table, signal, raw, spectra, table_sem, signal_sem, power_sem, out_sem) = refs[:n], refs[n:]
    segs, _, width = signal.shape
    nbins = table.shape[0] // 2
    rows = 2 * segs
    bins = BW // seg
    table_copy = pltpu.make_async_copy(table_hbm, table, table_sem)
    signal_copies = [pltpu.make_async_copy(signal_hbm.at[s], signal.at[s], signal_sem.at[s]) for s in range(segs)]
    power_copy = pltpu.make_async_copy(early_hbm.at[pl.ds(early_hbm.shape[0] - 1, 1)], spectra.at[pl.ds(nbins, 1)], power_sem)
    table_copy.start()
    power_copy.start()
    for copy in signal_copies:
        copy.start()
    table_copy.wait()
    power_copy.wait()
    for copy in signal_copies:
        copy.wait()
    for s in range(segs):
        spectrum = jnp.dot(table[...], signal[s], preferred_element_type=jnp.float32)
        for r in range(2):
            for h in range(width // LANES):
                raw[h, pl.ds(r * segs + s, nbins, stride=rows), :] = spectrum[r * nbins : (r + 1) * nbins, h * LANES : (h + 1) * LANES]
    for h in range(width // LANES):
        spectra[:nbins, :, h * LANES : (h + 1) * LANES] = raw[h, : nbins * rows].reshape(nbins, rows, LANES).astype(jnp.bfloat16)
    copies = []
    for (pairs, lent, shift, powered), out in zip(plan, outs):
        pieces = [(first_bin(band_ref, pair, lent, shift, seg), bins) for pair in pairs] + [(nbins, 1)] * powered
        for i, (start, size) in enumerate(pieces):
            copies.append(pltpu.make_async_copy(spectra.at[pl.ds(start, size)], out.at[pl.ds(i * bins, size)], out_sem.at[len(copies)]))
    for copy in copies:
        copy.start()
    for copy in copies:
        copy.wait()


def message_shape(message, bins, rows, width):
    pairs, _, _, powered = message
    return jax.ShapeDtypeStruct((len(pairs) * bins + powered, rows, width), jnp.bfloat16)


def make_spectra(plan, seg, band, table, signal, early):
    segs, length, width = signal.shape
    rows, bins, n, nbins = 2 * segs, BW // seg, len(plan), table.shape[0] // 2
    anywhere = pl.BlockSpec(memory_space=pl.ANY)
    return pl.pallas_call(
        functools.partial(spectra_kernel, plan, seg),
        in_specs=[pl.BlockSpec(memory_space=pltpu.SMEM)] + [anywhere] * 3,
        out_specs=[anywhere] * n,
        out_shape=[message_shape(m, bins, rows, width) for m in plan],
        scratch_shapes=[
            pltpu.VMEM(table.shape, jnp.bfloat16),
            pltpu.VMEM(signal.shape, jnp.bfloat16),
            pltpu.VMEM((width // LANES, (nbins + 1) * rows, LANES), jnp.float32),
            pltpu.VMEM((nbins + 1, rows, width), jnp.bfloat16),
            pltpu.SemaphoreType.DMA,
            pltpu.SemaphoreType.DMA((segs,)),
            pltpu.SemaphoreType.DMA,
            pltpu.SemaphoreType.DMA((sum(len(m[0]) + m[3] for m in plan),)),
        ],
        compiler_params=pltpu.CompilerParams(vmem_limit_bytes=56 << 20),
        cost_estimate=pl.CostEstimate(flops=2 * table.size * segs * width, bytes_accessed=32 << 20, transcendentals=0),
    )(band, table, signal, early)


def turned(y):
    half = y.shape[0] // 2
    return jnp.concatenate([-y[half:], y[:half]], axis=0)


def inv_rms_of(tiles, samples):
    power = 0.0
    for tile in tiles:
        t = tile.astype(jnp.float32)
        power = power + (t[0:1] + t[1:2] + t[2:3])
    return lax.rsqrt(power / samples + 1e-06)


def chunks_of(bins, lead, trail):
    sizes = [min(CHUNK, bins - f) for f in range(0, bins, CHUNK)]
    if lead and sizes[0] > 2:
        sizes[:1] = [2, sizes[0] - 2]
    if trail and sizes[-1] > 2:
        sizes[-1:] = [sizes[-1] - sizes[-1] // 2, sizes[-1] // 2]
    return [(sum(sizes[:c]), size) for c, size in enumerate(sizes)]


def cross_kernel(pairs, loads, samples, scale, sched_hbm, *refs):
    *arrays, out, sched_ref, held, ring, weight, sched_sem, in_sem, out_sem = refs
    sched_copy = pltpu.make_async_copy(sched_hbm, sched_ref, sched_sem)
    sched_copy.start()
    width = held.shape[-1]
    depth = ring.shape[1]
    chunks = [chunks_of(out.shape[3], i == 0, i == len(pairs) - 1) for i in range(len(pairs))]
    in_copies, out_copies, zero_copies = {}, [], []
    for load in loads:
        for array, first, size, slot in sum(load, []):
            if slot not in in_copies:
                in_copies[slot] = pltpu.make_async_copy(arrays[array].at[pl.ds(first, size)], held.at[slot, pl.ds(0, size)], in_sem.at[slot])
    for i, pair in enumerate(pairs):
        for slots, copies in ((depth, out_copies), (1, zero_copies)):
            copies.append(
                [
                    [
                        pltpu.make_async_copy(
                            ring.at[i, c % slots, r, pl.ds(0, size)], out.at[0, pair, r, pl.ds(first, size)], out_sem.at[i, c, r]
                        )
                        for r in range(2)
                    ]
                    for c, (first, size) in enumerate(chunks[i])
                ]
            )
    fresh, known = [], set()
    for load in loads:
        fresh.append([slot for *_, slot in sum(load, []) if slot not in known])
        fresh[-1] = list(dict.fromkeys(fresh[-1]))
        known.update(fresh[-1])
    for slot in fresh[0]:
        in_copies[slot].start()
    sched_copy.wait()
    for i, pair in enumerate(pairs):
        x_loads, y_loads, x_power, y_power = ([slot for _, _, _, slot in part] for part in loads[i])
        for slot in fresh[i]:
            in_copies[slot].wait()
        for slot in fresh[i + 1] if i + 1 < len(pairs) else []:
            in_copies[slot].start()
        live = sched_ref[0, pair]

        @pl.when(live == 0)
        def _(i=i):
            ring[i, 0] = jnp.zeros(ring.shape[2:], ring.dtype)
            for copy in sum(zero_copies[i], []):
                copy.start()
            for copy in sum(zero_copies[i][:-depth], []):
                copy.wait()

        @pl.when(live != 0)
        def _(i=i, x_loads=x_loads, y_loads=y_loads, x_power=x_power, y_power=y_power):
            by_row = jnp.broadcast_to(inv_rms_of([held[k, 0] for k in x_power], samples) * scale, (width, width)).T
            weight[...] = by_row * inv_rms_of([held[k, 0] for k in y_power], samples)
            for c, (first, size) in enumerate(chunks[i]):
                if c >= depth:
                    for copy in out_copies[i][c - depth]:
                        copy.wait()
                for f in range(first, first + size):
                    x = jnp.concatenate([held[k, f] for k in x_loads], axis=0)
                    y = jnp.concatenate([held[k, f] for k in y_loads], axis=0)
                    y_turned = jnp.concatenate([turned(held[k, f]) for k in y_loads], axis=0)
                    partner = jnp.concatenate([y, y_turned], axis=1)
                    product = lax.dot_general(x, partner, (((0,), (0,)), ((), ())), preferred_element_type=jnp.float32)
                    for r in range(2):
                        part = product[:, r * width : (r + 1) * width] * weight[...]
                        ring[i, c % depth, r, f - first] = part.astype(ring.dtype)
                for copy in out_copies[i][c]:
                    copy.start()

    for copies in out_copies:
        for copy in sum(copies[-depth:], []):
            copy.wait()


def cross(pairs, seg, samples, scale, sched, windows, powers, shape, out):
    bins, width = shape[3], shape[4]
    arrays, slots, loads = [], {}, []

    def load(array, first, size):
        known = [k for k, other in enumerate(arrays) if other is array]
        if not known:
            arrays.append(array)
        where = (known[0] if known else len(arrays) - 1, first, size)
        return (*where, slots.setdefault(where, len(slots)))

    for pair in pairs:
        x, y = ([load(*windows[pair, lent, k], bins) for k in range(seg)] for lent in (False, pair > 0))
        tiles = [[powers[p, lent, k] for k in range(seg)] for p, lent in ((0, False), (pair, pair > 0))]
        loads.append([x, y] + [[load(array, array.shape[0] - 1, 1) for array in part] for part in tiles])
    rows, kept = arrays[0].shape[1], windows[0, False, 0][0]
    anywhere, in_hbm = pl.BlockSpec(memory_space=pl.ANY), pl.BlockSpec(memory_space=pltpu.HBM)
    operands = [sched, *arrays]
    aliases = {}
    if out is not None:
        aliases = {len(operands): 0}
        operands.append(out)
    kernel = functools.partial(cross_kernel, pairs, loads, samples, scale)
    if out is not None:
        kernel = functools.partial(drop_ref, len(operands) - 1, kernel)
    return pl.pallas_call(
        kernel,
        in_specs=[in_hbm if a is sched or a is kept else anywhere for a in operands],
        out_specs=anywhere,
        scratch_shapes=[
            pltpu.SMEM(sched.shape, jnp.int32),
            pltpu.VMEM((len(slots), bins, rows, width), jnp.bfloat16),
            pltpu.VMEM((len(pairs), 3, 2, min(CHUNK, bins), width, width), jnp.bfloat16),
            pltpu.VMEM((width, width), jnp.float32),
            pltpu.SemaphoreType.DMA,
            pltpu.SemaphoreType.DMA((len(slots),)),
            pltpu.SemaphoreType.DMA((len(pairs), bins // min(CHUNK, bins) + 2, 2)),
        ],
        out_shape=jax.ShapeDtypeStruct(shape, jnp.bfloat16),
        input_output_aliases=aliases,
        compiler_params=pltpu.CompilerParams(vmem_limit_bytes=CROSS_VMEM),
        cost_estimate=pl.CostEstimate(
            flops=4 * len(pairs) * bins * seg * rows * width * width,
            bytes_accessed=4 * len(pairs) * bins * width * width,
            transcendentals=0,
        ),
    )(*operands)


def drop_ref(k, kernel, *refs):
    return kernel(*refs[:k], *refs[k + 1 :])


def body(signal, band, sched):
    seg_dev, length, width = signal.shape
    seg, chan = lax.axis_size("seg"), lax.axis_size("chan")
    segs = seg_dev * seg
    bins = BW // seg
    first, plan = message_plan(seg)
    table = dft_table(NB, length)
    cuts = early_spectra(first, seg, band.T, jnp.asarray(row_table(table)), signal)
    cuts += make_spectra(plan, seg, band.T, jnp.asarray(table), signal, cuts[0])

    def delivered(message, cut):
        pairs, lent, shift, _ = message
        away = pairs[0] if lent else 0
        if not away and not shift:
            return cut
        route = [(c * seg + s, (c - away) % chan * seg + (s + shift) % seg) for c in range(chan) for s in range(seg)]
        return lax.ppermute(cut, ("chan", "seg"), route)

    windows, powers = {}, {}
    scale = 1.0 / (segs * 0.375 * length) / LIFT**2
    shape = (1, PAIRS, 2, bins, width, width)
    out = None

    def deliver(message, cut, out=None):
        if out is not None:
            cut, out = lax.optimization_barrier((cut, out))
        pairs, lent, shift, powered = message
        array = delivered(message, cut)
        for i, pair in enumerate(pairs):
            windows[pair, lent, shift] = array, i * bins
            if powered:
                powers[pair, lent, shift] = array
        return out

    cuts = dict(zip(first + plan, cuts))
    for message, cut in cuts.items():
        if comes_after(message) is None:
            deliver(message, cut)
    for pairs in GROUPS:
        out = cross(pairs, seg, segs * length, scale, sched, windows, powers, shape, out)
        for message, cut in cuts.items():
            if comes_after(message) == pairs[-1]:
                out = deliver(message, cut, out)
    return out


def solution(mesh):
    in_specs = (P("seg", None, "chan"), P(), P("chan", None))
    out_specs = P("chan", None, None, "seg", None, None)
    return jax.shard_map(body, mesh=mesh, in_specs=in_specs, out_specs=out_specs, check_vma=False)
```
